32 devices in a mesh: row: 4 (over y, x), col: 8 (over z, core).
Axes of the slice: x: 2, y: 2, z: 4, core: 2. Of those that a mesh axis runs over, the one named last changes fastest.
Arguments:
- factor: float32 [4096, 4096], P('row', 'col'), may hold values from -7 to 12
Outputs:
- factor_next: float32 [4096, 4096], P('row', 'col')
The draws below stay inside these ranges and needn't reach their ends.
All inputs are finite; a program needn't handle non-finite values.
Results may differ from the reference program's by a relative error of at most 0.0078.
Values may be sent and summed in bfloat16 or wider, within the bound.
A program may use at most 64 MiB of HBM per device.

```python
import math
import jax
import jax.numpy as jnp
import numpy as np
from jax import lax

BLK = 256
SWEEPS = 2
STEPS = 2
ORDER = 4096
N_COL = 8


def draw_factor(key, part):
    key_noise = jax.random.fold_in(key, 11)
    key_diag = jax.random.fold_in(key, 12)
    key_scale = jax.random.fold_in(key, 13)
    noise_part = jnp.clip(1.8 * jax.random.normal(key_noise, (ORDER, ORDER), jnp.float32), -4.2, 4.2)
    scales = jax.random.uniform(key_scale, (ORDER,), jnp.float32, 0.95, 1.05)
    diagonal_part = jax.random.uniform(key_diag, (ORDER,), jnp.float32, 1.0, 3.0)
    symmetric = (noise_part + noise_part.T) * 0.7071 + jnp.eye(ORDER, dtype=jnp.float32) * diagonal_part[None, :]
    return symmetric * scales[:, None] * scales[None, :]


def setup_inputs(seed: int = 0) -> dict:
    key_list = jax.random.split(jax.random.key(seed), 2)
    factor = draw_factor(jax.random.fold_in(key_list[1], 71), 0)
    return dict(factor=factor)


def inner_solve(pair_block):
    size = pair_block.shape[0]
    weights = (jnp.arange(size, dtype=jnp.float32) + 1.0) / size
    step_size = 0.5 / math.sqrt(size)
    identity = jnp.eye(size, dtype=jnp.float32)
    rotation = identity
    current = pair_block
    for sweep_index in range(SWEEPS):
        skew_part = current * weights[None, :] - weights[:, None] * current
        trial_map = identity + step_size * skew_part
        gram_matrix = jnp.dot(trial_map.T, trial_map, precision=lax.Precision.HIGHEST)
        update = jnp.dot(trial_map, 1.5 * identity - 0.5 * gram_matrix, precision=lax.Precision.HIGHEST)
        current = jnp.dot(update.T, jnp.dot(current, update, precision=lax.Precision.HIGHEST), precision=lax.Precision.HIGHEST)
        rotation = jnp.dot(rotation, update, precision=lax.Precision.HIGHEST)
    return rotation

def half_sources(pair_count):
    upper = [0, 1] + [2 * (pair_index - 1) for pair_index in range(2, pair_count)]
    lower = [2 * (pair_index + 1) + 1 for pair_index in range(pair_count - 1)] + [2 * (pair_count - 1)]
    merged = []
    for pair_index in range(pair_count):
        merged += [upper[pair_index], lower[pair_index]]
    return np.array(merged)

def reference(factor):
    pair_count = N_COL
    pair_width = 2 * BLK
    sources = half_sources(pair_count)
    order_index = (sources[:, None] * BLK + np.arange(BLK)[None, :]).reshape(-1)
    matrix = factor
    for outer_step in range(STEPS):
        span = jnp.arange(pair_count)
        diagonals = matrix.reshape(pair_count, pair_width, pair_count, pair_width)[span, :, span, :]
        rotations = lax.map(inner_solve, diagonals).astype(jnp.bfloat16)
        rot_wide = rotations.astype(jnp.float32)
        lowered = matrix.astype(jnp.bfloat16).astype(jnp.float32).reshape(ORDER, pair_count, pair_width)
        right = jnp.einsum('ika,kab->ikb', lowered, rot_wide, precision=lax.Precision.HIGHEST)
        right = right.astype(jnp.bfloat16).astype(jnp.float32).reshape(pair_count, pair_width, ORDER)
        rotated = jnp.einsum('kab,kaj->kbj', rot_wide, right, precision=lax.Precision.HIGHEST)
        rotated = rotated.reshape(ORDER, ORDER)
        rotated = jnp.take(rotated, order_index, axis=0)
        matrix = jnp.take(rotated, order_index, axis=1)
    return matrix
```

```python
import functools
import math

import jax
import jax.numpy as jnp
from jax import lax
from jax.experimental import pallas as pl
from jax.experimental.pallas import tpu as pltpu
from jax.sharding import PartitionSpec as P

SWEEPS = 2
STEPS = 2
CHUNKS = 4
MESH = pl.DeviceIdType.MESH


def product(left, right):
    return jnp.dot(left, right, preferred_element_type=jnp.float32)


def product_t(left, right):
    return lax.dot_general(left, right, (((0,), (0,)), ((), ())), preferred_element_type=jnp.float32)


def inner_solve(pair_block):
    size = pair_block.shape[0]
    down = lax.broadcasted_iota(jnp.int32, (size, size), 0)
    across = lax.broadcasted_iota(jnp.int32, (size, size), 1)
    weight_gap = (across - down).astype(jnp.float32) * (0.5 / math.sqrt(size) / size)
    current = pair_block
    rest = None
    for sweep_index in range(SWEEPS):
        trial = current * weight_gap
        trial_low = trial.astype(jnp.bfloat16)
        excess = trial + trial.T + product_t(trial_low, trial_low)
        update = trial - 0.5 * (excess + product(trial_low, excess.astype(jnp.bfloat16)))
        update_low = update.astype(jnp.bfloat16)
        if sweep_index + 1 < SWEEPS:
            half_turned = current + product(current.astype(jnp.bfloat16), update_low)
            current = half_turned + product_t(update_low, half_turned.astype(jnp.bfloat16))
        if rest is None:
            rest = update
        else:
            rest = rest + update + product(rest.astype(jnp.bfloat16), update_low)
    return rest + jnp.where(down == across, 1.0, 0.0)


def kernel(row_count, pair_count, x_ref, o_ref, colr, rowr, gout, gin, hout, hin,
           in_sem, csend, crecv, rsend, rrecv, gsend, grecv, hsend, hrecv):
    width = o_ref.shape[1]
    half = width // 2
    group = o_ref.shape[0] // width
    chunk = width // CHUNKS
    bits = row_count.bit_length() - 1
    row = lax.axis_index("row")
    col = lax.axis_index("col")
    owner_row = col // group
    on_diag = row == owner_row
    slot = col % group
    sibling = col + 1 - 2 * (col % 2)

    load = pltpu.make_async_copy(x_ref, o_ref, in_sem)
    load.start()
    barrier = pltpu.get_barrier_semaphore()
    for offset in range(1, row_count):
        pl.semaphore_signal(barrier, inc=1, device_id={"row": (row + offset) % row_count},
                            device_id_type=MESH)
    for offset in (-2, -1, 1, 2):
        @pl.when((col + offset >= 0) & (col + offset < pair_count))
        def _():
            pl.semaphore_signal(barrier, inc=1, device_id={"col": col + offset}, device_id_type=MESH)
    peers = row_count - 1
    for offset in (-2, -1, 1, 2):
        peers += jnp.where((col + offset >= 0) & (col + offset < pair_count), 1, 0)
    pl.semaphore_wait(barrier, peers)
    load.wait()

    def remote(src, dst, send, recv, where):
        return pltpu.make_async_remote_copy(src_ref=src, dst_ref=dst, send_sem=send, recv_sem=recv,
                                            device_id=where, device_id_type=MESH)

    def act(cond, copy, what):
        @pl.when(cond)
        def _():
            getattr(copy, what)()

    def row_bit(index, bit):
        return (index // (1 << bit)) % 2

    def col_copies(step, q):
        piece = colr.at[step, pl.ds(q * chunk, chunk)]
        order = [(q + i) % bits for i in range(bits)]
        apart = [(row_bit(row, b) + row_bit(owner_row, b)) % 2 for b in order]
        out = []
        for i, b in enumerate(order):
            partner = row + (1 - 2 * row_bit(row, b)) * (1 << b)
            out.append((sum(apart[i:]) == 0,
                        remote(piece, piece, csend.at[step, q, i], crecv.at[step, q], {"row": partner})))
        return out

    def row_copies(step, j, q):
        piece = rowr.at[step, j, pl.ds(q * chunk, chunk)]
        owner = group * row + j
        lane = (col % 2) == (owner % 2)
        recv = rrecv.at[step, j, q]
        return [
            (lane & (col >= owner) & (col + 2 < pair_count),
             remote(piece, piece, rsend.at[step, j, q, 0], recv, {"col": col + 2})),
            (lane & (col <= owner) & (col >= 2),
             remote(piece, piece, rsend.at[step, j, q, 1], recv, {"col": col - 2})),
            (lane, remote(piece, piece, rsend.at[step, j, q, 2], recv, {"col": sibling})),
        ]

    def g_copies(step, j):
        rows = pl.ds(j * width, width)
        return [
            (col + 1 < pair_count,
             remote(gout.at[step, 0, rows], gin.at[step, 0, rows], gsend.at[step, j, 0],
                    grecv.at[step, j, 0], {"col": col + 1})),
            (col > 0,
             remote(gout.at[step, 1, rows], gin.at[step, 1, rows], gsend.at[step, j, 1],
                    grecv.at[step, j, 1], {"col": col - 1})),
        ]

    def h_copies(step):
        return [
            (row + 1 < row_count,
             remote(hout.at[step, 0], hin.at[step, 0], hsend.at[step, 0], hrecv.at[step, 0],
                    {"row": row + 1})),
            (row > 0,
             remote(hout.at[step, 1], hin.at[step, 1], hsend.at[step, 1], hrecv.at[step, 1],
                    {"row": row - 1})),
        ]

    def run(copies, what):
        for cond, copy in copies:
            act(cond, copy, what)

    def relay_col(step, q):
        copies = col_copies(step, q)
        @pl.when(jnp.logical_not(on_diag))
        def _():
            copies[0][1].wait_recv()
            run(copies, "start")

    def relay_row(step, q):
        for j in range(group):
            copies = row_copies(step, j, q)
            @pl.when(col != group * row + j)
            def _():
                copies[2][1].wait_recv()
                run(copies, "start")

    def one_step(step, carry):
        @pl.when(on_diag)
        def _():
            rotation = inner_solve(o_ref[pl.ds(pl.multiple_of(slot * width, width), width), :])
            colr[step] = rotation.astype(jnp.bfloat16)
            for q in range(CHUNKS):
                run(col_copies(step, q), "start")
            rowr[step, slot] = rotation.T.astype(jnp.bfloat16)
            for q in range(CHUNKS):
                for j in range(group):
                    @pl.when(slot == j)
                    def _():
                        run(row_copies(step, j, q), "start")

        for q in range(CHUNKS):
            relay_col(step, q)
            if q + 1 < CHUNKS:
                relay_row(step, q)

        for j in range(group):
            rows = pl.ds(j * width, width)
            right = product(o_ref[rows, :].astype(jnp.bfloat16), colr[step])
            upper = right[:, :half]
            lower = right[:, half:].astype(jnp.bfloat16)
            upper_low = upper.astype(jnp.bfloat16)
            gout[step, 1, rows] = lower

            @pl.when(col == 0)
            def _():
                gout[step, 0, rows] = lower
                gin[step, 0, rows] = upper_low

            @pl.when(col > 0)
            def _():
                gout[step, 0, rows] = upper_low

            @pl.when(col == pair_count - 1)
            def _():
                gin[step, 1, rows] = upper_low

            run(g_copies(step, j), "start")
        relay_row(step, CHUNKS - 1)

        for j in [0, group - 1] + list(range(1, group - 1)):
            rows = pl.ds(j * width, width)
            copies = g_copies(step, j)
            act(col > 0, copies[0][1], "wait_recv")
            act(col + 1 < pair_count, copies[1][1], "wait_recv")
            left = rowr[step, j]
            upper_rows = []
            for side in range(2):
                rotated = product(left, gin[step, side, rows])
                cols = pl.ds(side * half, half)
                upper = rotated[:half]
                lower = rotated[half:]

                def put(index, block):
                    o_ref[pl.ds(index * half, half), cols] = block

                if j == 0:
                    @pl.when(row == 0)
                    def _():
                        put(0, upper)
                        put(2, lower)

                    @pl.when(row > 0)
                    def _():
                        put(2, upper)
                        hout[step, 1, :, cols] = lower.astype(jnp.bfloat16)
                else:
                    put(2 * j - 1, lower)
                    if j < group - 1:
                        put(2 * j + 2, upper)
                    else:
                        @pl.when(row == row_count - 1)
                        def _():
                            put(2 * j + 1, upper)

                        @pl.when(row < row_count - 1)
                        def _():
                            hout[step, 0, :, cols] = upper.astype(jnp.bfloat16)
            if j == 0:
                run(h_copies(step)[1:], "start")
            elif j == group - 1:
                run(h_copies(step)[:1], "start")

        copies = h_copies(step)

        @pl.when(row < row_count - 1)
        def _():
            copies[1][1].wait_recv()
            o_ref[pl.ds((2 * group - 1) * half, half), :] = hin[step, 1].astype(jnp.float32)

        @pl.when(row > 0)
        def _():
            copies[0][1].wait_recv()
            o_ref[pl.ds(0, half), :] = hin[step, 0].astype(jnp.float32)

        for q in range(CHUNKS):
            run(col_copies(step, q), "wait_send")
            for j in range(group):
                run(row_copies(step, j, q), "wait_send")
        for j in range(group):
            run(g_copies(step, j), "wait_send")
        run(copies, "wait_send")
        return carry

    lax.fori_loop(0, STEPS, one_step, 0)


def shards(factor):
    rows, width = factor.shape
    half = width // 2
    group = rows // width
    row_count = lax.axis_size("row")
    pair_count = lax.axis_size("col")
    bits = row_count.bit_length() - 1
    low = jnp.bfloat16
    dma = pltpu.SemaphoreType.DMA
    return pl.pallas_call(
        functools.partial(kernel, row_count, pair_count),
        out_shape=jax.ShapeDtypeStruct(factor.shape, factor.dtype),
        in_specs=[pl.BlockSpec(memory_space=pl.ANY)],
        out_specs=pl.BlockSpec(memory_space=pltpu.VMEM),
        scratch_shapes=[
            pltpu.VMEM((STEPS, width, width), low),
            pltpu.VMEM((STEPS, group, width, width), low),
            pltpu.VMEM((STEPS, 2, rows, half), low),
            pltpu.VMEM((STEPS, 2, rows, half), low),
            pltpu.VMEM((STEPS, 2, half, width), low),
            pltpu.VMEM((STEPS, 2, half, width), low),
            dma,
            dma((STEPS, CHUNKS, bits)),
            dma((STEPS, CHUNKS)),
            dma((STEPS, group, CHUNKS, 3)),
            dma((STEPS, group, CHUNKS)),
            dma((STEPS, group, 2)),
            dma((STEPS, group, 2)),
            dma((STEPS, 2)),
            dma((STEPS, 2)),
        ],
        compiler_params=pltpu.CompilerParams(
            collective_id=0, has_side_effects=True, vmem_limit_bytes=56 * 1024 * 1024
        ),
    )(factor)


def solution(mesh):
    spec = P("row", "col")
    return jax.shard_map(shards, mesh=mesh, in_specs=(spec,), out_specs=spec, check_vma=False)
```

```python
import functools
import math

import jax
import jax.numpy as jnp
from jax import lax
from jax.experimental import pallas as pl
from jax.experimental.pallas import tpu as pltpu
from jax.sharding import PartitionSpec as P

SWEEPS = 2
STEPS = 2
CHUNKS = 4
PARTS = 1
MESH = pl.DeviceIdType.MESH


def product(left, right):
    return jnp.dot(left, right, preferred_element_type=jnp.float32)


def product_t(left, right):
    return lax.dot_general(left, right, (((0,), (0,)), ((), ())), preferred_element_type=jnp.float32)


def inner_solve(pair_block):
    size = pair_block.shape[0]
    down = lax.broadcasted_iota(jnp.int32, (size, size), 0)
    across = lax.broadcasted_iota(jnp.int32, (size, size), 1)
    weight_gap = (across - down).astype(jnp.float32) * (0.5 / math.sqrt(size) / size)
    current = pair_block
    rest = None
    for sweep_index in range(SWEEPS):
        trial = current * weight_gap
        trial_low = trial.astype(jnp.bfloat16)
        excess = trial + trial.T + product_t(trial_low, trial_low)
        update = trial - 0.5 * (excess + product(trial_low, excess.astype(jnp.bfloat16)))
        update_low = update.astype(jnp.bfloat16)
        if sweep_index + 1 < SWEEPS:
            half_turned = current + product(current.astype(jnp.bfloat16), update_low)
            current = half_turned + product_t(update_low, half_turned.astype(jnp.bfloat16))
        if rest is None:
            rest = update
        else:
            rest = rest + update + product(rest.astype(jnp.bfloat16), update_low)
    return rest + jnp.where(down == across, 1.0, 0.0)


def kernel(row_count, pair_count, x_ref, o_ref, colr, rowr, gout, gin, hout, hin,
           in_sem, csend, crecv, rsend, rrecv, tsend, trecv, gsend, grecv, hsend, hrecv):
    width = o_ref.shape[1]
    half = width // 2
    group = o_ref.shape[0] // width
    chunk = width // CHUNKS
    parts = csend.shape[1]
    part = width // parts
    bits = row_count.bit_length() - 1
    row = lax.axis_index("row")
    col = lax.axis_index("col")
    owner_row = col // group
    on_diag = row == owner_row
    slot = col % group
    sibling = col + 1 - 2 * (col % 2)

    load = pltpu.make_async_copy(x_ref, o_ref, in_sem)
    load.start()
    barrier = pltpu.get_barrier_semaphore()
    for offset in range(1, row_count):
        pl.semaphore_signal(barrier, inc=1, device_id={"row": (row + offset) % row_count},
                            device_id_type=MESH)
    for offset in (-2, -1, 1, 2):
        @pl.when((col + offset >= 0) & (col + offset < pair_count))
        def _():
            pl.semaphore_signal(barrier, inc=1, device_id={"col": col + offset}, device_id_type=MESH)
    peers = row_count - 1
    for offset in (-2, -1, 1, 2):
        peers += jnp.where((col + offset >= 0) & (col + offset < pair_count), 1, 0)

    def remote(src, dst, send, recv, where):
        return pltpu.make_async_remote_copy(src_ref=src, dst_ref=dst, send_sem=send, recv_sem=recv,
                                            device_id=where, device_id_type=MESH)

    def act(cond, copy, what):
        @pl.when(cond)
        def _():
            getattr(copy, what)()

    def row_bit(index, bit):
        return (index // (1 << bit)) % 2

    def col_copies(step, q):
        piece = colr.at[step, pl.ds(q * part, part)]
        order = [(q + i) % bits for i in range(bits)]
        apart = [(row_bit(row, b) + row_bit(owner_row, b)) % 2 for b in order]
        out = []
        for i, b in enumerate(order):
            partner = row + (1 - 2 * row_bit(row, b)) * (1 << b)
            out.append((sum(apart[i:]) == 0,
                        remote(piece, piece, csend.at[step, q, i], crecv.at[step, q], {"row": partner})))
        return out

    def on_lane(j):
        return (col % 2) == ((group * row + j) % 2)

    def row_copies(step, j, q):
        piece = rowr.at[step, j, pl.ds(q * chunk, chunk)]
        owner = group * row + j
        recv = rrecv.at[step, j, q]
        return [
            (on_lane(j) & (col >= owner) & (col + 2 < pair_count),
             remote(piece, piece, rsend.at[step, j, q, 0], recv, {"col": col + 2})),
            (on_lane(j) & (col <= owner) & (col >= 2),
             remote(piece, piece, rsend.at[step, j, q, 1], recv, {"col": col - 2})),
        ]

    def twin_copy(step, j):
        piece = rowr.at[step, j]
        return remote(piece, piece, tsend.at[step, j], trecv.at[step, j], {"col": sibling})

    def g_copies(step, j):
        rows = pl.ds(j * width, width)
        return [
            (col + 1 < pair_count,
             remote(gout.at[step, 0, rows], gin.at[step, 0, rows], gsend.at[step, j, 0],
                    grecv.at[step, j, 0], {"col": col + 1})),
            (col > 0,
             remote(gout.at[step, 1, rows], gin.at[step, 1, rows], gsend.at[step, j, 1],
                    grecv.at[step, j, 1], {"col": col - 1})),
        ]

    def h_copies(step):
        return [
            (row + 1 < row_count,
             remote(hout.at[step, 0], hin.at[step, 0], hsend.at[step, 0], hrecv.at[step, 0],
                    {"row": row + 1})),
            (row > 0,
             remote(hout.at[step, 1], hin.at[step, 1], hsend.at[step, 1], hrecv.at[step, 1],
                    {"row": row - 1})),
        ]

    def run(copies, what):
        for cond, copy in copies:
            act(cond, copy, what)

    def relay_col(step):
        for q in range(parts):
            copies = col_copies(step, q)
            @pl.when(jnp.logical_not(on_diag) & copies[-1][0])
            def _():
                copies[0][1].wait_recv()
                run(copies, "start")

    def settle_col(step):
        for q in range(parts):
            copies = col_copies(step, q)
            @pl.when(jnp.logical_not(on_diag | copies[-1][0]))
            def _():
                copies[0][1].wait_recv()

    def relay_row(step, q):
        for j in range(group):
            copies = row_copies(step, j, q)
            @pl.when(on_lane(j) & (col != group * row + j))
            def _():
                copies[0][1].wait_recv()
                run(copies, "start")
                if q == CHUNKS - 1:
                    twin_copy(step, j).start()

    def receive_rows(step):
        copies = h_copies(step)

        @pl.when(row < row_count - 1)
        def _():
            copies[1][1].wait_recv()
            o_ref[pl.ds((2 * group - 1) * half, half), :] = hin[step, 1].astype(jnp.float32)

        @pl.when(row > 0)
        def _():
            copies[0][1].wait_recv()
            o_ref[pl.ds(0, half), :] = hin[step, 0].astype(jnp.float32)

    def solve(step):
        rotation = inner_solve(o_ref[pl.ds(pl.multiple_of(slot * width, width), width), :])
        colr[step] = rotation.astype(jnp.bfloat16)
        rowr[step, slot] = rotation.T.astype(jnp.bfloat16)

    load.wait()

    @pl.when(on_diag)
    def _():
        solve(0)

    pl.semaphore_wait(barrier, peers)

    def one_step(step, carry):
        @pl.when(on_diag)
        def _():
            for i in range(bits):
                for q in range(parts):
                    col_copies(step, q)[i][1].start()
            for j in range(group):
                @pl.when(slot == j)
                def _():
                    for q in range(CHUNKS):
                        run(row_copies(step, j, q), "start")
                    twin_copy(step, j).start()

        relay_col(step)
        for q in range(CHUNKS - 1):
            relay_row(step, q)
        settle_col(step)

        @pl.when((step > 0) & jnp.logical_not(on_diag))
        def _():
            receive_rows(step - 1)

        for j in range(group):
            rows = pl.ds(j * width, width)
            right = product(o_ref[rows, :].astype(jnp.bfloat16), colr[step])
            upper = right[:, :half]
            lower = right[:, half:].astype(jnp.bfloat16)
            upper_low = upper.astype(jnp.bfloat16)
            gout[step, 1, rows] = lower

            @pl.when(col == 0)
            def _():
                gout[step, 0, rows] = lower
                gin[step, 0, rows] = upper_low

            @pl.when(col > 0)
            def _():
                gout[step, 0, rows] = upper_low

            @pl.when(col == pair_count - 1)
            def _():
                gin[step, 1, rows] = upper_low

            run(g_copies(step, j), "start")
        relay_row(step, CHUNKS - 1)
        for j in range(group):
            @pl.when(jnp.logical_not(on_lane(j)))
            def _():
                twin_copy(step, j).wait_recv()

        for j in [0, group - 1] + list(range(1, group - 1)):
            rows = pl.ds(j * width, width)
            copies = g_copies(step, j)
            act(col > 0, copies[0][1], "wait_recv")
            act(col + 1 < pair_count, copies[1][1], "wait_recv")
            left = rowr[step, j]
            upper_rows = []
            for side in range(2):
                rotated = product(left, gin[step, side, rows])
                cols = pl.ds(side * half, half)
                upper = rotated[:half]
                lower = rotated[half:]

                def put(index, block):
                    o_ref[pl.ds(index * half, half), cols] = block

                if j == 0:
                    @pl.when(row == 0)
                    def _():
                        put(0, upper)
                        put(2, lower)

                    @pl.when(row > 0)
                    def _():
                        put(2, upper)
                        hout[step, 1, :, cols] = lower.astype(jnp.bfloat16)
                else:
                    put(2 * j - 1, lower)
                    if j < group - 1:
                        put(2 * j + 2, upper)
                    else:
                        @pl.when(row == row_count - 1)
                        def _():
                            put(2 * j + 1, upper)

                        @pl.when(row < row_count - 1)
                        def _():
                            hout[step, 0, :, cols] = upper.astype(jnp.bfloat16)
            if j == 0:
                run(h_copies(step)[1:], "start")
            elif j == group - 1:
                run(h_copies(step)[:1], "start")

        @pl.when((step < STEPS - 1) & on_diag)
        def _():
            receive_rows(step)
            solve(step + 1)

        return carry

    lax.fori_loop(0, STEPS, one_step, 0)
    receive_rows(STEPS - 1)

    def drain(step, carry):
        for q in range(parts):
            run(col_copies(step, q), "wait_send")
        for j in range(group):
            for q in range(CHUNKS):
                run(row_copies(step, j, q), "wait_send")
            act(on_lane(j), twin_copy(step, j), "wait_send")
            run(g_copies(step, j), "wait_send")
        run(h_copies(step), "wait_send")
        return carry

    lax.fori_loop(0, STEPS, drain, 0)


def shards(factor):
    rows, width = factor.shape
    half = width // 2
    group = rows // width
    row_count = lax.axis_size("row")
    pair_count = lax.axis_size("col")
    bits = row_count.bit_length() - 1
    low = jnp.bfloat16
    parts = PARTS * (1 << (bits - 1).bit_length())
    dma = pltpu.SemaphoreType.DMA
    return pl.pallas_call(
        functools.partial(kernel, row_count, pair_count),
        out_shape=jax.ShapeDtypeStruct(factor.shape, factor.dtype),
        in_specs=[pl.BlockSpec(memory_space=pl.ANY)],
        out_specs=pl.BlockSpec(memory_space=pltpu.VMEM),
        scratch_shapes=[
            pltpu.VMEM((STEPS, width, width), low),
            pltpu.VMEM((STEPS, group, width, width), low),
            pltpu.VMEM((STEPS, 2, rows, half), low),
            pltpu.VMEM((STEPS, 2, rows, half), low),
            pltpu.VMEM((STEPS, 2, half, width), low),
            pltpu.VMEM((STEPS, 2, half, width), low),
            dma,
            dma((STEPS, parts, bits)),
            dma((STEPS, parts)),
            dma((STEPS, group, CHUNKS, 2)),
            dma((STEPS, group, CHUNKS)),
            dma((STEPS, group)),
            dma((STEPS, group)),
            dma((STEPS, group, 2)),
            dma((STEPS, group, 2)),
            dma((STEPS, 2)),
            dma((STEPS, 2)),
        ],
        compiler_params=pltpu.CompilerParams(
            collective_id=0, has_side_effects=True, vmem_limit_bytes=56 * 1024 * 1024
        ),
    )(factor)


def solution(mesh):
    spec = P("row", "col")
    return jax.shard_map(shards, mesh=mesh, in_specs=(spec,), out_specs=spec, check_vma=False)
```

```python
import functools
import math

import jax
import jax.numpy as jnp
from jax import lax
from jax.experimental import pallas as pl
from jax.experimental.pallas import tpu as pltpu
from jax.sharding import PartitionSpec as P

SWEEPS = 2
STEPS = 2
CHUNKS = 8
PARTS = 1
MESH = pl.DeviceIdType.MESH


def product(left, right):
    return jnp.dot(left, right, preferred_element_type=jnp.float32)


def product_t(left, right):
    return lax.dot_general(left, right, (((0,), (0,)), ((), ())), preferred_element_type=jnp.float32)


def inner_solve(pair_block):
    size = pair_block.shape[0]
    down = lax.broadcasted_iota(jnp.int32, (size, size), 0)
    across = lax.broadcasted_iota(jnp.int32, (size, size), 1)
    weight_gap = (across - down).astype(jnp.float32) * (0.5 / math.sqrt(size) / size)
    current = pair_block
    rest = None
    for sweep_index in range(SWEEPS):
        trial = current * weight_gap
        trial_low = trial.astype(jnp.bfloat16)
        excess = trial + trial.T + product_t(trial_low, trial_low)
        update = trial - 0.5 * (excess + product(trial_low, excess.astype(jnp.bfloat16)))
        update_low = update.astype(jnp.bfloat16)
        if sweep_index + 1 < SWEEPS:
            half_turned = current + product(current.astype(jnp.bfloat16), update_low)
            current = half_turned + product_t(update_low, half_turned.astype(jnp.bfloat16))
        if rest is None:
            rest = update
        else:
            rest = rest + update + product(rest.astype(jnp.bfloat16), update_low)
    return rest + jnp.where(down == across, 1.0, 0.0)


def kernel(row_count, pair_count, x_ref, o_ref, colr, rowr, gout, gin, hout, hin,
           in_sem, csend, crecv, rsend, rrecv, tsend, trecv, gsend, grecv, hsend, hrecv):
    width = o_ref.shape[1]
    half = width // 2
    group = o_ref.shape[0] // width
    chunk = width // CHUNKS
    parts = csend.shape[1]
    part = width // parts
    bits = row_count.bit_length() - 1
    row = lax.axis_index("row")
    col = lax.axis_index("col")
    owner_row = col // group
    on_diag = row == owner_row
    slot = col % group
    sibling = col + 1 - 2 * (col % 2)

    load = pltpu.make_async_copy(x_ref, o_ref, in_sem)
    load.start()
    barrier = pltpu.get_barrier_semaphore()
    for offset in range(1, row_count):
        pl.semaphore_signal(barrier, inc=1, device_id={"row": (row + offset) % row_count},
                            device_id_type=MESH)
    for offset in (-2, -1, 1, 2):
        @pl.when((col + offset >= 0) & (col + offset < pair_count))
        def _():
            pl.semaphore_signal(barrier, inc=1, device_id={"col": col + offset}, device_id_type=MESH)
    peers = row_count - 1
    for offset in (-2, -1, 1, 2):
        peers += jnp.where((col + offset >= 0) & (col + offset < pair_count), 1, 0)

    def remote(src, dst, send, recv, where):
        return pltpu.make_async_remote_copy(src_ref=src, dst_ref=dst, send_sem=send, recv_sem=recv,
                                            device_id=where, device_id_type=MESH)

    def act(cond, copy, what):
        @pl.when(cond)
        def _():
            getattr(copy, what)()

    def row_bit(index, bit):
        return (index // (1 << bit)) % 2

    def col_copies(step, q):
        piece = colr.at[step, pl.ds(q * part, part)]
        order = [(q + i) % bits for i in range(bits)]
        apart = [(row_bit(row, b) + row_bit(owner_row, b)) % 2 for b in order]
        out = []
        for i, b in enumerate(order):
            partner = row + (1 - 2 * row_bit(row, b)) * (1 << b)
            out.append((sum(apart[i:]) == 0,
                        remote(piece, piece, csend.at[step, q, i], crecv.at[step, q], {"row": partner})))
        return out

    def on_lane(j):
        return (col % 2) == ((group * row + j) % 2)

    def row_copies(step, j, q):
        piece = rowr.at[step, j, pl.ds(q * chunk, chunk)]
        owner = group * row + j
        recv = rrecv.at[step, j, q]
        return [
            (on_lane(j) & (col >= owner) & (col + 2 < pair_count),
             remote(piece, piece, rsend.at[step, j, q, 0], recv, {"col": col + 2})),
            (on_lane(j) & (col <= owner) & (col >= 2),
             remote(piece, piece, rsend.at[step, j, q, 1], recv, {"col": col - 2})),
        ]

    def twin_copy(step, j):
        piece = rowr.at[step, j]
        return remote(piece, piece, tsend.at[step, j], trecv.at[step, j], {"col": sibling})

    def g_copies(step, j):
        rows = pl.ds(j * width, width)
        return [
            (col + 1 < pair_count,
             remote(gout.at[step, 0, rows], gin.at[step, 0, rows], gsend.at[step, j, 0],
                    grecv.at[step, j, 0], {"col": col + 1})),
            (col > 0,
             remote(gout.at[step, 1, rows], gin.at[step, 1, rows], gsend.at[step, j, 1],
                    grecv.at[step, j, 1], {"col": col - 1})),
        ]

    def h_copies(step, side):
        return [
            (row + 1 < row_count,
             remote(hout.at[step, 0, side], hin.at[step, 0, side], hsend.at[step, 0, side],
                    hrecv.at[step, 0, side], {"row": row + 1})),
            (row > 0,
             remote(hout.at[step, 1, side], hin.at[step, 1, side], hsend.at[step, 1, side],
                    hrecv.at[step, 1, side], {"row": row - 1})),
        ]

    def run(copies, what):
        for cond, copy in copies:
            act(cond, copy, what)

    def relay_col(step):
        for q in range(parts):
            copies = col_copies(step, q)
            @pl.when(jnp.logical_not(on_diag) & copies[-1][0])
            def _():
                copies[0][1].wait_recv()
                run(copies, "start")

    def settle_col(step):
        for q in range(parts):
            copies = col_copies(step, q)
            @pl.when(jnp.logical_not(on_diag | copies[-1][0]))
            def _():
                copies[0][1].wait_recv()

    def relay_row(step, q):
        for j in range(group):
            copies = row_copies(step, j, q)
            @pl.when(on_lane(j) & (col != group * row + j))
            def _():
                copies[0][1].wait_recv()
                run(copies, "start")
                if q == CHUNKS - 1:
                    twin_copy(step, j).start()

    def receive_rows(step):
        for side in range(2):
            copies = h_copies(step, side)
            cols = pl.ds(side * half, half)

            @pl.when(row < row_count - 1)
            def _():
                copies[1][1].wait_recv()
                o_ref[pl.ds((2 * group - 1) * half, half), cols] = hin[step, 1, side].astype(jnp.float32)

            @pl.when(row > 0)
            def _():
                copies[0][1].wait_recv()
                o_ref[pl.ds(0, half), cols] = hin[step, 0, side].astype(jnp.float32)

    def solve(step):
        rotation = inner_solve(o_ref[pl.ds(pl.multiple_of(slot * width, width), width), :])
        colr[step] = rotation.astype(jnp.bfloat16)
        rowr[step, slot] = rotation.T.astype(jnp.bfloat16)

    load.wait()

    @pl.when(on_diag)
    def _():
        solve(0)

    pl.semaphore_wait(barrier, peers)

    def one_step(step, carry):
        @pl.when(on_diag)
        def _():
            for i in range(bits):
                for q in range(parts):
                    col_copies(step, q)[i][1].start()
            for j in range(group):
                @pl.when(slot == j)
                def _():
                    for q in range(CHUNKS):
                        run(row_copies(step, j, q), "start")
                    twin_copy(step, j).start()

        relay_col(step)
        for q in range(CHUNKS - 1):
            relay_row(step, q)
        settle_col(step)

        @pl.when((step > 0) & jnp.logical_not(on_diag))
        def _():
            receive_rows(step - 1)

        for j in range(group):
            rows = pl.ds(j * width, width)
            right = product(o_ref[rows, :].astype(jnp.bfloat16), colr[step])
            upper = right[:, :half]
            lower = right[:, half:].astype(jnp.bfloat16)
            upper_low = upper.astype(jnp.bfloat16)
            gout[step, 1, rows] = lower

            @pl.when(col == 0)
            def _():
                gout[step, 0, rows] = lower
                gin[step, 0, rows] = upper_low

            @pl.when(col > 0)
            def _():
                gout[step, 0, rows] = upper_low

            @pl.when(col == pair_count - 1)
            def _():
                gin[step, 1, rows] = upper_low

            run(g_copies(step, j), "start")
        relay_row(step, CHUNKS - 1)
        for j in range(group):
            @pl.when(jnp.logical_not(on_lane(j)))
            def _():
                twin_copy(step, j).wait_recv()

        for j in [0, group - 1] + list(range(1, group - 1)):
            rows = pl.ds(j * width, width)
            copies = g_copies(step, j)
            act(col > 0, copies[0][1], "wait_recv")
            act(col + 1 < pair_count, copies[1][1], "wait_recv")
            left = rowr[step, j]
            upper_rows = []
            for side in range(2):
                rotated = product(left, gin[step, side, rows])
                cols = pl.ds(side * half, half)
                upper = rotated[:half]
                lower = rotated[half:]

                def put(index, block):
                    o_ref[pl.ds(index * half, half), cols] = block

                if j == 0:
                    @pl.when(row == 0)
                    def _():
                        put(0, upper)
                        put(2, lower)

                    @pl.when(row > 0)
                    def _():
                        put(2, upper)
                        hout[step, 1, side] = lower.astype(jnp.bfloat16)
                else:
                    put(2 * j - 1, lower)
                    if j < group - 1:
                        put(2 * j + 2, upper)
                    else:
                        @pl.when(row == row_count - 1)
                        def _():
                            put(2 * j + 1, upper)

                        @pl.when(row < row_count - 1)
                        def _():
                            hout[step, 0, side] = upper.astype(jnp.bfloat16)
                if j == 0:
                    run(h_copies(step, side)[1:], "start")
                elif j == group - 1:
                    run(h_copies(step, side)[:1], "start")

        @pl.when((step < STEPS - 1) & on_diag)
        def _():
            receive_rows(step)
            solve(step + 1)

        return carry

    lax.fori_loop(0, STEPS, one_step, 0)
    receive_rows(STEPS - 1)

    def drain(step, carry):
        for q in range(parts):
            run(col_copies(step, q), "wait_send")
        for j in range(group):
            for q in range(CHUNKS):
                run(row_copies(step, j, q), "wait_send")
            act(on_lane(j), twin_copy(step, j), "wait_send")
            run(g_copies(step, j), "wait_send")
        for side in range(2):
            run(h_copies(step, side), "wait_send")
        return carry

    lax.fori_loop(0, STEPS, drain, 0)


def shards(factor):
    rows, width = factor.shape
    half = width // 2
    group = rows // width
    row_count = lax.axis_size("row")
    pair_count = lax.axis_size("col")
    bits = row_count.bit_length() - 1
    low = jnp.bfloat16
    parts = PARTS * (1 << (bits - 1).bit_length())
    dma = pltpu.SemaphoreType.DMA
    return pl.pallas_call(
        functools.partial(kernel, row_count, pair_count),
        out_shape=jax.ShapeDtypeStruct(factor.shape, factor.dtype),
        in_specs=[pl.BlockSpec(memory_space=pl.ANY)],
        out_specs=pl.BlockSpec(memory_space=pltpu.VMEM),
        scratch_shapes=[
            pltpu.VMEM((STEPS, width, width), low),
            pltpu.VMEM((STEPS, group, width, width), low),
            pltpu.VMEM((STEPS, 2, rows, half), low),
            pltpu.VMEM((STEPS, 2, rows, half), low),
            pltpu.VMEM((STEPS, 2, 2, half, half), low),
            pltpu.VMEM((STEPS, 2, 2, half, half), low),
            dma,
            dma((STEPS, parts, bits)),
            dma((STEPS, parts)),
            dma((STEPS, group, CHUNKS, 2)),
            dma((STEPS, group, CHUNKS)),
            dma((STEPS, group)),
            dma((STEPS, group)),
            dma((STEPS, group, 2)),
            dma((STEPS, group, 2)),
            dma((STEPS, 2, 2)),
            dma((STEPS, 2, 2)),
        ],
        compiler_params=pltpu.CompilerParams(
            collective_id=0, has_side_effects=True, vmem_limit_bytes=24 * 1024 * 1024
        ),
    )(factor)


def solution(mesh):
    spec = P("row", "col")
    return jax.shard_map(shards, mesh=mesh, in_specs=(spec,), out_specs=spec, check_vma=False)
```
